32 devices in a mesh: groups: 2 (over x), gx: 16 (over z, y, core).
Axes of the slice: x: 2, y: 2, z: 4, core: 2. Of those that a mesh axis runs over, the one named last changes fastest.
Arguments:
- fine_frequency: float32 [32, 3, 64], P(('groups', 'gx')), parts along dimension 0, may hold values from -8 to 8
- fine_weights: float32 [32, 2, 128, 128], P(('groups', 'gx')), parts along dimension 0, may hold values from -1 to 1
- fine_biases: float32 [32, 2, 128], P(('groups', 'gx')), parts along dimension 0, may hold values from -3 to 3
- fine_readout: float32 [32, 128], P(('groups', 'gx')), parts along dimension 0, may hold values from -0.5 to 0.5
- block_frequency: float32 [2, 3, 64], P('groups'), parts along dimension 0, may hold values from -8 to 8
- block_weights: float32 [2, 2, 128, 128], P('groups'), parts along dimension 0, may hold values from -1 to 1
- block_biases: float32 [2, 2, 128], P('groups'), parts along dimension 0, may hold values from -3 to 3
- block_readout: float32 [2, 128], P('groups'), parts along dimension 0, may hold values from -0.5 to 0.5
- whole_frequency: float32 [6, 64], P('groups'), parts along dimension 0, may hold values from -8 to 8
- whole_weights: float32 [4, 128, 128], P('groups'), parts along dimension 0, may hold values from -1 to 1
- whole_biases: float32 [4, 128], P('groups'), parts along dimension 0, may hold values from -3 to 3
- whole_readout: float32 [256], P('groups'), parts along dimension 0, may hold values from -0.5 to 0.5
- speed_table: float32 [16], replicated, may hold values from 0.5 to 2
- speed_field: int32 [1024, 1024], P(('groups', 'gx')), parts along dimension 0, may hold values from 0 to 15
- point_cells: int32 [32, 256], P(('groups', 'gx')), parts along dimension 0, may hold values from 0 to 32767, as said below
- margin_points: int32 [32, 2, 32], P(('groups', 'gx')), parts along dimension 0, may hold values from 0 to 255, as said below
- source: float32 [32, 256], P(('groups', 'gx')), parts along dimension 0, may hold values from -68 to 68
Outputs:
- fine_frequency_grad: float32 [32, 3, 64], P(('groups', 'gx')), parts along dimension 0
- fine_weights_grad: float32 [32, 2, 128, 128], P(('groups', 'gx')), parts along dimension 0
- fine_biases_grad: float32 [32, 2, 128], P(('groups', 'gx')), parts along dimension 0
- fine_readout_grad: float32 [32, 128], P(('groups', 'gx')), parts along dimension 0
- block_frequency_grad: float32 [2, 3, 64], P('groups'), parts along dimension 0
- block_weights_grad: float32 [2, 2, 128, 128], P('groups'), parts along dimension 0
- block_biases_grad: float32 [2, 2, 128], P('groups'), parts along dimension 0
- block_readout_grad: float32 [2, 128], P('groups'), parts along dimension 0
- whole_frequency_grad: float32 [6, 64], P('groups'), parts along dimension 0
- whole_weights_grad: float32 [4, 128, 128], P('groups'), parts along dimension 0
- whole_biases_grad: float32 [4, 128], P('groups'), parts along dimension 0
- whole_readout_grad: float32 [256], P('groups'), parts along dimension 0
The draws below stay inside these ranges and needn't reach their ends.
There are 2 independent parts, one for each index of `groups`. The reference program is written for one: setup_inputs(seed, part) draws one part's arguments, and reference() takes and returns one part's arrays. A program takes and returns all parts, laid end to end along the dimension named above; an argument that names none is the same for every part. Nothing has to cross between parts.
Inputs may be any that keep to these rules, and one draw needn't show every extreme that they name: point_cells[d, p] = i * 32 * 32 + j * 32 + k names a cell of subdomain d's lattice; exactly the points listed in margin_points[d, 0] have i < 4, exactly those in margin_points[d, 1] have i >= 28. The 64 entries of margin_points[d] are distinct points of subdomain d.
All inputs are finite; a program needn't handle non-finite values.
Results may differ from the reference program's by a relative error of at most 0.0003.
Values sent between devices are 32-bit elements; how exact they have to be, the bound alone decides.
A program may use at most 128 MiB of HBM per device.

```python
import math
import jax
import jax.numpy as jnp
from jax import lax

UNITS = 128
FREQS = 64
LAYERS = 2
PTS = 256
STRIP_PTS = 32
GRID = 32
STRIP = 4
BLOCK = 16
NSPEED = 16
NSUB = 16
NBLK = 1


def strip_layout(key):

    def one_subdomain(sub_key):
        perm_key, depth_key, face_key = jax.random.split(sub_key, 3)
        ordering = jax.random.permutation(perm_key, PTS).astype(jnp.int32)
        ordering = jnp.roll(ordering, -jnp.argmax(ordering == PTS - 1))
        slot_index = jnp.arange(PTS, dtype=jnp.int32)
        layer_floor = jnp.where(slot_index < STRIP_PTS, 0, jnp.where(slot_index < 2 * STRIP_PTS, GRID - STRIP, STRIP))
        layer_span = jnp.where(slot_index < 2 * STRIP_PTS, STRIP, GRID - 2 * STRIP)
        depth_draw = layer_floor + jax.random.randint(depth_key, (PTS,), 0, 1 << 20, dtype=jnp.int32) % layer_span
        face_cell = jax.random.randint(face_key, (PTS,), 0, GRID * GRID, dtype=jnp.int32)
        placed = depth_draw * GRID * GRID + face_cell
        placed = placed.at[0].set(0).at[STRIP_PTS].set(GRID * GRID * GRID - 1)
        cell_ids = jnp.zeros((PTS,), jnp.int32).at[ordering].set(placed)
        return (cell_ids, ordering[:2 * STRIP_PTS].reshape(2, STRIP_PTS))
    return jax.vmap(one_subdomain)(jax.random.split(key, NSUB))


def draw_point_cells(key, part):
    cell_ids, listed = strip_layout(key)
    return cell_ids


def draw_margin_points(key, part):
    cell_ids, listed = strip_layout(key)
    return listed


def draw_source(key, part):
    key = jax.random.fold_in(key, 7)
    first_key, second_key = jax.random.split(key, 2)
    placement = jnp.arange(NSUB, dtype=jnp.float32)[:, None] / max(NSUB - 1, 1)
    noise_draw = jnp.clip(jax.random.normal(first_key, (NSUB, PTS), jnp.float32), -5.0, 5.0)
    trend_factor = 1.0 + 2.0 * placement
    spread = jnp.exp(jax.random.uniform(second_key, (NSUB, PTS), jnp.float32, 0.0, 2.3))
    return noise_draw * trend_factor * spread * 0.3


def set_ends(values, key, smallest, largest):
    shape = values.shape
    index_at = [jax.random.randint(jax.random.fold_in(key, axis), (), 0, shape[axis]) for axis in range(len(shape))]
    values = values.at[tuple(index_at)].set(smallest)
    longest = shape.index(max(shape))
    index_at[longest] = (index_at[longest] + 1) % shape[longest]
    return values.at[tuple(index_at)].set(largest)


def block_scale(stream_key, shape, cuts, least, top_value):
    def one(dim, blocks):
        steps = jax.random.uniform(jax.random.fold_in(jax.random.fold_in(stream_key, 6), dim), (blocks,), jnp.float32, least / len(cuts), top_value / len(cuts))
        return jnp.repeat(jnp.exp(steps), shape[dim] // blocks).reshape((-1,) + (1,) * (len(shape) - dim - 1))

    factor_of = one(*cuts[0])
    for cut in cuts[1:]:
        factor_of = factor_of * one(*cut)
    return factor_of


def scatter_about(rng, extent, scale, reach, cuts=(), kind=jnp.bfloat16):
    loudness = block_scale(rng, extent, cuts, -0.22, 0.18) if cuts else 1.0
    result = jax.random.normal(rng, extent, jnp.float32) * scale * loudness
    return jnp.minimum(jnp.maximum(result, -reach), reach).astype(kind)


def setup_inputs(seed: int = 0, part: int = 0) -> dict:
    key_list = jax.random.split(jax.random.key(seed), 18)
    part_keys = jax.random.split(jax.random.fold_in(key_list[17], part), 18)
    fine_frequency = scatter_about(part_keys[0], (NSUB, 3, FREQS), 1.8, 8.0, ((0, 16),), jnp.float32)
    fine_weights = scatter_about(part_keys[1], (NSUB, LAYERS, UNITS, UNITS), (UNITS // 4) ** -0.5, 1.0, ((0, 16),), jnp.float32)
    fine_biases = scatter_about(part_keys[2], (NSUB, LAYERS, UNITS), 0.5, 3.0, ((0, 16),), jnp.float32)
    fine_readout = scatter_about(part_keys[3], (NSUB, UNITS), UNITS ** -0.5, 0.5, ((0, 16),), jnp.float32)
    block_frequency = scatter_about(part_keys[4], (NBLK, 3, FREQS), 1.8, 8.0, (), jnp.float32)
    block_weights = scatter_about(part_keys[5], (NBLK, LAYERS, UNITS, UNITS), (UNITS // 4) ** -0.5, 1.0, (), jnp.float32)
    block_biases = scatter_about(part_keys[6], (NBLK, LAYERS, UNITS), 0.5, 3.0, (), jnp.float32)
    block_readout = scatter_about(part_keys[7], (NBLK, UNITS), UNITS ** -0.5, 0.5, (), jnp.float32)
    whole_frequency = scatter_about(part_keys[8], (3, FREQS), 1.8, 8.0, (), jnp.float32)
    whole_weights = scatter_about(part_keys[9], (LAYERS, UNITS, UNITS), (UNITS // 4) ** -0.5, 1.0, (), jnp.float32)
    whole_biases = scatter_about(part_keys[10], (LAYERS, UNITS), 0.5, 3.0, (), jnp.float32)
    whole_readout = scatter_about(part_keys[11], (UNITS,), UNITS ** -0.5, 0.5, (), jnp.float32)
    speed_table = jnp.clip(jnp.exp(jax.random.uniform(key_list[12], (NSPEED,), jnp.float32, math.log(0.5), math.log(2.0))), 0.5, 2.0)
    speed_field = set_ends(jax.random.randint(part_keys[13], (NSUB * GRID, GRID * GRID), 0, NSPEED), jax.random.fold_in(part_keys[13], 1), 0, NSPEED - 1).astype(jnp.int32)
    point_cells = draw_point_cells(jax.random.fold_in(jax.random.fold_in(key_list[17], part), 71), part)
    margin_points = draw_margin_points(jax.random.fold_in(jax.random.fold_in(key_list[17], part), 71), part)
    source = draw_source(jax.random.fold_in(jax.random.fold_in(key_list[17], part), 71), part)
    return {"fine_frequency": fine_frequency, "fine_weights": fine_weights, "fine_biases": fine_biases, "fine_readout": fine_readout, "block_frequency": block_frequency, "block_weights": block_weights, "block_biases": block_biases, "block_readout": block_readout, "whole_frequency": whole_frequency, "whole_weights": whole_weights, "whole_biases": whole_biases, "whole_readout": whole_readout, "speed_table": speed_table, "speed_field": speed_field, "point_cells": point_cells, "margin_points": margin_points, "source": source}


kappa = 3.125
epsilon = 1e-06
highest = lax.Precision.HIGHEST

def network(params, points):
    frequency, weights, biases, readout = params
    unit_count = readout.shape[0]
    point_count = points.shape[0]
    phases = jnp.dot(points, frequency, precision=highest, preferred_element_type=jnp.float32)
    sines = jnp.sin(phases)
    cosines = jnp.cos(phases)
    squared = lax.optimization_barrier(jnp.sum(frequency * frequency, axis=0))
    channels = [jnp.concatenate([sines, cosines], axis=1)]
    for axis_pick in range(3):
        channels.append(jnp.concatenate([cosines * frequency[axis_pick], -sines * frequency[axis_pick]], axis=1))
    channels.append(jnp.concatenate([-sines * squared, -cosines * squared], axis=1))
    jets = jnp.stack(channels)
    for section_index in range(weights.shape[0]):
        mixture = jnp.dot(jets.reshape(-1, unit_count), weights[section_index], precision=highest, preferred_element_type=jnp.float32).reshape(5, point_count, unit_count)
        active = jnp.tanh(mixture[0] + biases[section_index])
        derivative = 1.0 - active * active
        second = -2.0 * active * derivative
        gradients = derivative * mixture[1:4]
        curvature = derivative * mixture[4] + second * lax.optimization_barrier(jnp.sum(mixture[1:4] * mixture[1:4], axis=0))
        jets = jnp.concatenate([active[None], gradients, curvature[None]], axis=0)
    output = jnp.dot(jets.reshape(-1, unit_count), readout, precision=highest, preferred_element_type=jnp.float32).reshape(5, point_count)
    return (output[0], output[1], output[4])

def smooth_ramp(position):
    inside = (position > 0.0) & (position < 1.0)
    clipped = jnp.clip(position, 0.0, 1.0)
    height = 0.5 - 0.5 * jnp.cos(jnp.pi * clipped)
    slopes = jnp.where(inside, 0.5 * jnp.pi * jnp.sin(jnp.pi * clipped), 0.0)
    curvature = jnp.where(inside, 0.5 * jnp.pi * jnp.pi * jnp.cos(jnp.pi * clipped), 0.0)
    return (height, slopes, curvature)

def window(abscissa, lower_edge, upper_edge, margin):
    inverse_width = 0.5 / margin
    rise_height, rise_slope, rise_curve = smooth_ramp((abscissa - lower_edge + margin) * inverse_width)
    fall_height, fall_slope, fall_curve = smooth_ramp((upper_edge + margin - abscissa) * inverse_width)
    height = rise_height * fall_height
    slopes = inverse_width * (rise_slope * fall_height - rise_height * fall_slope)
    curvature = inverse_width * inverse_width * (rise_curve * fall_height - 2.0 * rise_slope * fall_slope + rise_height * fall_curve)
    return (height, slopes, curvature)

def windowed(params, points, lower_edge, upper_edge, margin):
    net_value, along_first, net_laplace = network(params, points)
    height, slopes, curvature = window(points[:, 0], lower_edge, upper_edge, margin)
    return (height * net_value, height * net_laplace + 2.0 * slopes * along_first + curvature * net_value)

def locate(cell_ids, offset):
    depth_index = (cell_ids // (GRID * GRID)).astype(jnp.float32)
    row_index = (cell_ids // GRID % GRID).astype(jnp.float32)
    column = (cell_ids % GRID).astype(jnp.float32)
    return jnp.stack([offset + (depth_index + 0.5) / GRID, (row_index + 0.5) / GRID, (column + 0.5) / GRID], axis=1)

def reference(fine_frequency, fine_weights, fine_biases, fine_readout, block_frequency, block_weights, block_biases, block_readout, whole_frequency, whole_weights, whole_biases, whole_readout, speed_table, speed_field, point_cells, margin_points, source):
    margin = STRIP / GRID
    subdomain_ids = jnp.arange(NSUB, dtype=jnp.int32)
    offsets = subdomain_ids.astype(jnp.float32)
    points = jax.vmap(locate)(point_cells, offsets)
    flat_field = speed_field.reshape(NSUB, GRID * GRID * GRID)
    speed_codes = jax.vmap(lambda table_row, picks: table_row[picks])(flat_field, point_cells)
    speeds = speed_table[speed_codes]
    slowness = 1.0 / (speeds * speeds)
    left_ids = margin_points[:, 0]
    right_ids = margin_points[:, 1]
    gather_rows = jax.vmap(lambda source_rows, picks: source_rows[picks])
    left_points = gather_rows(points, left_ids)
    right_points = gather_rows(points, right_ids)
    home = subdomain_ids // BLOCK
    left_block = jnp.maximum(subdomain_ids - 1, 0) // BLOCK
    right_block = jnp.minimum(subdomain_ids + 1, NSUB - 1) // BLOCK
    has_left = (subdomain_ids > 0).astype(jnp.float32)[:, None]
    has_right = (subdomain_ids < NSUB - 1).astype(jnp.float32)[:, None]
    left_edge = ((subdomain_ids % BLOCK == 0) & (subdomain_ids > 0)).astype(jnp.float32)[:, None]
    right_edge = ((subdomain_ids % BLOCK == BLOCK - 1) & (subdomain_ids < NSUB - 1)).astype(jnp.float32)[:, None]
    per_subdomain = jax.vmap(windowed, in_axes=(0, 0, 0, 0, None))
    scatter_add = jax.vmap(lambda target, picks, extra: target.at[picks].add(extra))

    def pick_rows(params, picks):
        return jax.tree.map(lambda array: array[picks], params)

    def squared_sum(fine, block, whole):
        own_value, own_laplace = per_subdomain(fine, points, offsets, offsets + 1.0, margin)
        after = jax.tree.map(lambda array: jnp.roll(array, -1, axis=0), fine)
        before = jax.tree.map(lambda array: jnp.roll(array, 1, axis=0), fine)
        left_value, left_laplace = per_subdomain(before, left_points, offsets - 1.0, offsets, margin)
        right_value, right_laplace = per_subdomain(after, right_points, offsets + 1.0, offsets + 2.0, margin)
        home_floor = (home * BLOCK).astype(jnp.float32)
        home_value, home_laplace = per_subdomain(pick_rows(block, home), points, home_floor, home_floor + BLOCK, margin)
        left_floor = (left_block * BLOCK).astype(jnp.float32)
        lower_value, lower_laplace = per_subdomain(pick_rows(block, left_block), left_points, left_floor, left_floor + BLOCK, margin)
        right_floor = (right_block * BLOCK).astype(jnp.float32)
        upper_value, upper_laplace = per_subdomain(pick_rows(block, right_block), right_points, right_floor, right_floor + BLOCK, margin)
        whole_value, whole_along, whole_laplace = network(whole, points.reshape(-1, 3))
        field_value = own_value + home_value + whole_value.reshape(NSUB, PTS)
        field_laplace = own_laplace + home_laplace + whole_laplace.reshape(NSUB, PTS)
        field_value = scatter_add(field_value, left_ids, has_left * left_value + left_edge * lower_value)
        field_value = scatter_add(field_value, right_ids, has_right * right_value + right_edge * upper_value)
        field_laplace = scatter_add(field_laplace, left_ids, has_left * left_laplace + left_edge * lower_laplace)
        field_laplace = scatter_add(field_laplace, right_ids, has_right * right_laplace + right_edge * upper_laplace)
        residual = field_laplace / (kappa * kappa) + slowness * field_value - source
        return jnp.sum(residual * residual)
    power = jnp.mean(source * source) + epsilon
    fine_grad, block_grad, whole_grad = jax.grad(squared_sum, argnums=(0, 1, 2))((fine_frequency, fine_weights, fine_biases, fine_readout), (block_frequency, block_weights, block_biases, block_readout), (whole_frequency, whole_weights, whole_biases, whole_readout))
    scale = 1.0 / (2.0 * PTS * power)
    return (fine_grad[0] * scale, fine_grad[1] * scale, fine_grad[2] * scale, fine_grad[3] * scale, block_grad[0] * scale, block_grad[1] * scale, block_grad[2] * scale, block_grad[3] * scale, whole_grad[0] * scale, whole_grad[1] * scale, whole_grad[2] * scale, whole_grad[3] * scale)
```

```python
import functools

import jax
import jax.numpy as jnp
from jax import lax
from jax.experimental import pallas as pl
from jax.experimental.pallas import tpu as pltpu
from jax.sharding import PartitionSpec as P

GRID = 32
STRIP = 4
BLOCK = 16


kappa = 3.125
epsilon = 1e-06
highest = lax.Precision.HIGHEST


def with_halo(cells, sides, width):
    for axis, dim in sides:
        count = lax.axis_size(axis)
        ends = count - 1
        head = lax.slice_in_dim(cells, 0, width, axis=dim)
        tail = lax.slice_in_dim(cells, cells.shape[dim] - width, cells.shape[dim], axis=dim)
        cells = jnp.concatenate(
            [
                lax.ppermute(tail, axis, [(i, (i + 1) % count) for i in range(ends)]),
                cells,
                lax.ppermute(head, axis, [((i + 1) % count, i) for i in range(ends)]),
            ],
            axis=dim,
        )
    return cells


def network(params, points):
    frequency, weights, biases, readout = params
    unit_count = readout.shape[0]
    point_count = points.shape[0]
    phases = jnp.dot(points, frequency, precision=highest, preferred_element_type=jnp.float32)
    sines = jnp.sin(phases)
    cosines = jnp.cos(phases)
    squared = jnp.sum(frequency * frequency, axis=0)
    channels = [jnp.concatenate([sines, cosines], axis=1)]
    for axis_pick in range(3):
        channels.append(
            jnp.concatenate([cosines * frequency[axis_pick], -sines * frequency[axis_pick]], axis=1)
        )
    channels.append(jnp.concatenate([-sines * squared, -cosines * squared], axis=1))
    jets = jnp.stack(channels)
    for section_index in range(weights.shape[0]):
        mixture = jnp.dot(
            jets.reshape(-1, unit_count),
            weights[section_index],
            precision=highest,
            preferred_element_type=jnp.float32,
        ).reshape(5, point_count, unit_count)
        active = jnp.tanh(mixture[0] + biases[section_index])
        derivative = 1.0 - active * active
        second = -2.0 * active * derivative
        gradients = derivative * mixture[1:4]
        curvature = derivative * mixture[4] + second * jnp.sum(mixture[1:4] * mixture[1:4], axis=0)
        jets = jnp.concatenate([active[None], gradients, curvature[None]], axis=0)
    output = jnp.dot(
        jets.reshape(-1, unit_count), readout, precision=highest, preferred_element_type=jnp.float32
    ).reshape(5, point_count)
    return (output[0], output[1], output[4])


def smooth_ramp(position):
    inside = (position > 0.0) & (position < 1.0)
    clipped = jnp.clip(position, 0.0, 1.0)
    height = 0.5 - 0.5 * jnp.cos(jnp.pi * clipped)
    slopes = jnp.where(inside, 0.5 * jnp.pi * jnp.sin(jnp.pi * clipped), 0.0)
    curvature = jnp.where(inside, 0.5 * jnp.pi * jnp.pi * jnp.cos(jnp.pi * clipped), 0.0)
    return (height, slopes, curvature)


def window(abscissa, lower_edge, upper_edge, margin):
    inverse_width = 0.5 / margin
    rise_height, rise_slope, rise_curve = smooth_ramp(
        (abscissa - lower_edge + margin) * inverse_width
    )
    fall_height, fall_slope, fall_curve = smooth_ramp(
        (upper_edge + margin - abscissa) * inverse_width
    )
    height = rise_height * fall_height
    slopes = inverse_width * (rise_slope * fall_height - rise_height * fall_slope)
    curvature = (
        inverse_width
        * inverse_width
        * (rise_curve * fall_height - 2.0 * rise_slope * fall_slope + rise_height * fall_curve)
    )
    return (height, slopes, curvature)


def windowed(params, points, lower_edge, upper_edge, margin):
    net_value, along_first, net_laplace = network(params, points)
    height, slopes, curvature = window(points[:, 0], lower_edge, upper_edge, margin)
    return (
        height * net_value,
        height * net_laplace + 2.0 * slopes * along_first + curvature * net_value,
    )


def locate(cell_ids, offset):
    depth_index = (cell_ids // (GRID * GRID)).astype(jnp.float32)
    row_index = (cell_ids // GRID % GRID).astype(jnp.float32)
    column = (cell_ids % GRID).astype(jnp.float32)
    return jnp.stack(
        [offset + (depth_index + 0.5) / GRID, (row_index + 0.5) / GRID, (column + 0.5) / GRID],
        axis=1,
    )


def select_row(params, which):
    return jax.tree.map(lambda array: array[which], params)


def shards(
    fine_frequency,
    fine_weights,
    fine_biases,
    fine_readout,
    block_frequency,
    block_weights,
    block_biases,
    block_readout,
    whole_frequency,
    whole_weights,
    whole_biases,
    whole_readout,
    speed_table,
    speed_field,
    point_cells,
    margin_points,
    source,
):
    margin = STRIP / GRID
    device_index = lax.axis_index("gx")
    device_count = lax.axis_size("gx")
    offset = device_index.astype(jnp.float32)
    fine_own = (fine_frequency[0], fine_weights[0], fine_biases[0], fine_readout[0])
    block = (block_frequency, block_weights, block_biases, block_readout)
    whole = (whole_frequency, whole_weights, whole_biases, whole_readout)
    local_source = source[0]
    point_total = local_source.shape[0]
    strip_count = margin_points.shape[2]
    power_term = jnp.sum(local_source * local_source)
    power_total = lax.psum(power_term, "gx")
    cell_ids = point_cells[0]
    points = locate(cell_ids, offset)
    speed_codes = speed_field.reshape(-1)[cell_ids]
    table_levels = jnp.arange(speed_table.shape[0], dtype=jnp.int32)
    speeds = jnp.sum(
        jnp.where(speed_codes[:, None] == table_levels[None, :], speed_table[None, :], 0.0), axis=1
    )
    slowness = 1.0 / (speeds * speeds)
    left_ids = margin_points[0, 0]
    right_ids = margin_points[0, 1]
    left_points = points[left_ids]
    right_points = points[right_ids]
    home = device_index // BLOCK
    left_block = jnp.maximum(device_index - 1, 0) // BLOCK
    right_block = jnp.minimum(device_index + 1, device_count - 1) // BLOCK
    left_edge = ((device_index % BLOCK == 0) & (device_index > 0)).astype(jnp.float32)
    right_edge = ((device_index % BLOCK == BLOCK - 1) & (device_index < device_count - 1)).astype(
        jnp.float32
    )

    def shared_terms(fine_params, block_params, whole_params):
        own_value, own_laplace = windowed(fine_params, points, offset, offset + 1.0, margin)
        home_floor = (home * BLOCK).astype(jnp.float32)
        home_value, home_laplace = windowed(
            select_row(block_params, home), points, home_floor, home_floor + BLOCK, margin
        )
        left_floor = (left_block * BLOCK).astype(jnp.float32)
        lower_value, lower_laplace = windowed(
            select_row(block_params, left_block),
            left_points,
            left_floor,
            left_floor + BLOCK,
            margin,
        )
        right_floor = (right_block * BLOCK).astype(jnp.float32)
        upper_value, upper_laplace = windowed(
            select_row(block_params, right_block),
            right_points,
            right_floor,
            right_floor + BLOCK,
            margin,
        )
        whole_value, whole_along, whole_laplace = network(whole_params, points)
        return (
            own_value + home_value + whole_value,
            own_laplace + home_laplace + whole_laplace,
            left_edge * jnp.stack([lower_value, lower_laplace]),
            right_edge * jnp.stack([upper_value, upper_laplace]),
        )

    strip_coords = jnp.concatenate([left_points, right_points], axis=0).T
    padded = with_halo(strip_coords, (("gx", 1),), strip_count)
    guest_points = jnp.concatenate([padded[:, :strip_count], padded[:, -strip_count:]], axis=1).T

    def guest_terms(fine_params):
        guest_value, guest_laplace = windowed(
            fine_params, guest_points, offset, offset + 1.0, margin
        )
        return jnp.stack([guest_value, guest_laplace])

    guest_parts, guest_pull = jax.vjp(guest_terms, fine_own)
    arrived = with_halo(guest_parts, (("gx", 1),), strip_count)
    from_left = arrived[:, :strip_count]
    from_right = arrived[:, -strip_count:]
    (field_value, field_laplace, left_extra, right_extra), shared_pull = jax.vjp(
        shared_terms, fine_own, block, whole
    )
    left_total = left_extra + from_left
    right_total = right_extra + from_right
    field_value = field_value.at[left_ids].add(left_total[0]).at[right_ids].add(right_total[0])
    field_laplace = field_laplace.at[left_ids].add(left_total[1]).at[right_ids].add(right_total[1])
    residual = field_laplace / (kappa * kappa) + slowness * field_value - local_source
    value_weight = residual * slowness
    laplace_weight = residual / (kappa * kappa)
    left_cot = jnp.stack([value_weight[left_ids], laplace_weight[left_ids]])
    right_cot = jnp.stack([value_weight[right_ids], laplace_weight[right_ids]])
    fine_grad, block_grad, whole_grad = shared_pull(
        (value_weight, laplace_weight, left_cot, right_cot)
    )
    sent_back = jnp.concatenate([left_cot, right_cot], axis=1)
    returned = with_halo(sent_back, (("gx", 1),), strip_count)
    guest_cot = jnp.concatenate([returned[:, :strip_count], returned[:, -strip_count:]], axis=1)
    extra_grad = guest_pull(guest_cot)[0]
    fine_grad = jax.tree.map(
        lambda first_part, second_part: first_part + second_part, fine_grad, extra_grad
    )
    whole_sum = lax.psum((whole_grad[0], whole_grad[1], whole_grad[2], whole_grad[3]), "gx")
    block_sum = lax.psum((block_grad[0], block_grad[1], block_grad[2], block_grad[3]), "gx")
    power = power_total / (device_count * point_total) + epsilon
    scale = 1.0 / (point_total * power)
    return (
        fine_grad[0][None] * scale,
        fine_grad[1][None] * scale,
        fine_grad[2][None] * scale,
        fine_grad[3][None] * scale,
        block_sum[0] * scale,
        block_sum[1] * scale,
        block_sum[2] * scale,
        block_sum[3] * scale,
        whole_sum[0] * scale,
        whole_sum[1] * scale,
        whole_sum[2] * scale,
        whole_sum[3] * scale,
    )


BLK_ROWS = 16
f32 = jnp.float32
bf16 = jnp.bfloat16


def split(values):
    high = values.astype(bf16)
    return high, (values - high.astype(f32)).astype(bf16)


def nt_dot(first, second):
    return lax.dot_general(first, second, (((1,), (1,)), ((), ())), preferred_element_type=f32)


def sincos(angle):
    turns = jnp.floor(angle * 0.6366197723675814 + 0.5)
    quadrant = turns.astype(jnp.int32)
    rest = angle - turns * 1.5703125
    rest = rest - turns * 4.837512969970703125e-4
    rest = rest - turns * 7.54978995489188216e-8
    square = rest * rest
    sine = (-1.9515295891e-4 * square + 8.3321608736e-3) * square - 1.6666654611e-1
    sine = rest + rest * square * sine
    cosine = (2.443315711809948e-5 * square - 1.388731625493765e-3) * square + 4.166664568298827e-2
    cosine = 1.0 - 0.5 * square + square * square * cosine
    odd = (quadrant & 1) == 1
    first = jnp.where(odd, cosine, sine)
    second = jnp.where(odd, sine, cosine)
    first = jnp.where((quadrant & 2) == 2, -first, first)
    second = jnp.where(((quadrant + 1) & 2) == 2, -second, second)
    return first, second


def ramp_rows(position):
    inside = (position > 0.0) & (position < 1.0)
    sine, cosine = sincos(jnp.pi * jnp.clip(position, 0.0, 1.0))
    return (
        0.5 - 0.5 * cosine,
        jnp.where(inside, 0.5 * jnp.pi * sine, 0.0),
        jnp.where(inside, 0.5 * jnp.pi * jnp.pi * cosine, 0.0),
    )


def window_rows(abscissa, lower_edge, upper_edge):
    margin = STRIP / GRID
    inverse_width = 0.5 / margin
    rise, rise_slope, rise_curve = ramp_rows((abscissa - lower_edge + margin) * inverse_width)
    fall, fall_slope, fall_curve = ramp_rows((upper_edge + margin - abscissa) * inverse_width)
    return (
        rise * fall,
        inverse_width * (rise_slope * fall - rise * fall_slope),
        inverse_width
        * inverse_width
        * (rise_curve * fall - 2.0 * rise_slope * fall_slope + rise * fall_curve),
    )


def wide(column, width):
    return jnp.concatenate([column] * (width // 128), axis=1)


def stacked_row(row):
    high, low = split(row)
    high = high.astype(f32)
    low = low.astype(f32)
    top = jnp.concatenate([high, high], axis=1)
    bottom = jnp.concatenate([low, jnp.zeros_like(low)], axis=1)
    level = lax.broadcasted_iota(jnp.int32, (16, top.shape[1]), 0)
    return jnp.where(level == 0, top, jnp.where(level == 1, bottom, 0.0)).astype(bf16)


def two_rows(row):
    high, low = split(row)
    level = lax.broadcasted_iota(jnp.int32, (16, row.shape[1]), 0)
    return jnp.where(
        level == 0, high.astype(f32), jnp.where(level == 1, low.astype(f32), 0.0)
    ).astype(bf16)


def rows_at(step):
    return pl.ds(pl.multiple_of(step * BLK_ROWS, BLK_ROWS), BLK_ROWS)


def low_rows_at(step, start):
    return pl.ds(pl.multiple_of(step * BLK_ROWS + start, BLK_ROWS), BLK_ROWS)


def prepare_net(flip, columns, lifted, frequency, weights, biases, readout):
    flip[...] = jnp.zeros_like(flip)
    flip[0:2, :] = biases
    flip[2:3, :] = readout
    flip[3:6, 0:64] = frequency
    flip[3:6, 64:128] = frequency
    turned = flip[...].T
    parts = [jnp.broadcast_to(turned[:, k : k + 1], (128, 128)) for k in range(6)]
    for k in range(6):
        columns[k] = parts[k]
    columns[6] = parts[3] * parts[3] + parts[4] * parts[4] + parts[5] * parts[5]
    for layer in range(2):
        for which in range(2):
            matrix = weights[layer]
            high, low = split(matrix.T if which == 0 else matrix)
            lifted[layer, which, 0:128, 0:128] = high
            lifted[layer, which, 0:128, 128:256] = high
            lifted[layer, which, 128:256, 0:128] = low
            lifted[layer, which, 128:256, 128:256] = jnp.zeros_like(low)


def apply_lifted(matrix, stacked, result):
    for channel in range(5):
        product = jnp.dot(matrix, stacked[channel], preferred_element_type=f32)
        result[channel] = product[0:128] + product[128:256]


def store_split(target, channel, step, value, start=0):
    high, low = split(value)
    target[channel, low_rows_at(step, start), :] = high
    target[channel, low_rows_at(step, start + 128), :] = low


def forward(columns, lifted, waves, jets, mixes, readout, coords, width):
    along, across, upward = coords

    def lift(step, carry):
        rows = rows_at(step)
        freqs = [wide(columns[3 + k, rows, :], width) for k in range(3)]
        squared = wide(columns[6, rows, :], width)
        phase = along * freqs[0] + across * freqs[1] + upward * freqs[2]
        sine, cosine = sincos(phase)
        waves[0, rows, :] = sine
        waves[1, rows, :] = cosine
        store_split(jets[0], 0, step, sine)
        store_split(jets[0], 0, step, cosine, 64)
        for k in range(3):
            store_split(jets[0], 1 + k, step, cosine * freqs[k])
            store_split(jets[0], 1 + k, step, -sine * freqs[k], 64)
        store_split(jets[0], 4, step, -sine * squared)
        store_split(jets[0], 4, step, -cosine * squared, 64)
        return carry

    lax.fori_loop(0, 4, lift, 0)
    for layer in range(2):
        mix = mixes[layer]
        target = jets[layer + 1]
        apply_lifted(lifted[layer, 0], jets[layer], mix)

        def activate(step, carry):
            rows = rows_at(step)
            active = jnp.tanh(mix[0, rows, :] + wide(columns[layer, rows, :], width))
            derivative = 1.0 - active * active
            second = -2.0 * active * derivative
            m1, m2, m3, m4 = [mix[k, rows, :] for k in range(1, 5)]
            mix[0, rows, :] = active
            curvature = derivative * m4 + second * (m1 * m1 + m2 * m2 + m3 * m3)
            store_split(target, 0, step, active)
            store_split(target, 1, step, derivative * m1)
            if layer == 0:
                store_split(target, 2, step, derivative * m2)
                store_split(target, 3, step, derivative * m3)
                store_split(target, 4, step, curvature)
            else:
                store_split(target, 2, step, curvature)
            return carry

        lax.fori_loop(0, 8, activate, 0)
    left = stacked_row(readout)
    outs = []
    for channel in range(3):
        product = jnp.dot(left, jets[2][channel], preferred_element_type=f32)
        outs.append(product[0:1] + product[1:2])
    return outs


def backward(columns, lifted, waves, jets, mixes, back, cots, coords, alpha, beta, gamma, width, put):
    readout_rows = jnp.zeros((16, 256), f32)
    for channel, row in enumerate((alpha, beta, gamma)):
        readout_rows += nt_dot(two_rows(row), jets[2][channel])
    readout_rows = readout_rows[0:1] + readout_rows[1:2]
    put("readout", readout_rows[:, 0:128] + readout_rows[:, 128:256])
    ones = jnp.ones((16, width), bf16)
    for layer in (1, 0):
        mix = mixes[layer]

        def pull(step, carry):
            rows = rows_at(step)
            active = mix[0, rows, :]
            derivative = 1.0 - active * active
            second = -2.0 * active * derivative
            m = [mix[k, rows, :] for k in range(1, 5)]
            square = m[0] * m[0] + m[1] * m[1] + m[2] * m[2]
            if layer == 1:
                weight = wide(columns[2, rows, :], width)
                active_cot, curve_cot = weight * alpha, weight * gamma
                slope_cots = [weight * beta, None, None]
            else:
                active_cot, curve_cot = cots[0, rows, :], cots[4, rows, :]
                slope_cots = [cots[k, rows, :] for k in range(1, 4)]
            derivative_cot = curve_cot * m[3]
            for k in range(3):
                if slope_cots[k] is not None:
                    derivative_cot += slope_cots[k] * m[k]
            second_cot = curve_cot * square
            double = 2.0 * curve_cot * second
            store_split(back, 4, step, curve_cot * derivative)
            for k in range(3):
                value = double * m[k]
                if slope_cots[k] is not None:
                    value += slope_cots[k] * derivative
                store_split(back, 1 + k, step, value)
            derivative_cot = derivative_cot - 2.0 * active * second_cot
            active_cot = active_cot - 2.0 * (derivative * second_cot + active * derivative_cot)
            store_split(back, 0, step, active_cot * derivative)
            return carry

        lax.fori_loop(0, 8, pull, 0)
        bias_rows = nt_dot(ones, back[0])
        put(("bias", layer), bias_rows[0:1, 0:128] + bias_rows[0:1, 128:256])
        grad = jnp.zeros((256, 256), f32)
        for channel in range(5):
            grad += nt_dot(jets[layer][channel], back[channel])
        grad = grad[0:128] + grad[128:256]
        put(("weight", layer), grad[:, 0:128] + grad[:, 128:256])
        apply_lifted(lifted[layer, 1], back, cots)

    def sink(step, carry):
        rows = rows_at(step)
        later = low_rows_at(step, 64)
        sine, cosine = waves[0, rows, :], waves[1, rows, :]
        squared = wide(columns[6, rows, :], width)
        freqs = [wide(columns[3 + k, rows, :], width) for k in range(3)]
        phase_cot = cosine * cots[0, rows, :] - sine * cots[0, later, :]
        slopes = []
        for k in range(3):
            top, bottom = cots[1 + k, rows, :], cots[1 + k, later, :]
            phase_cot -= freqs[k] * (sine * top + cosine * bottom)
            slopes.append(cosine * top - sine * bottom)
        top, bottom = cots[4, rows, :], cots[4, later, :]
        phase_cot -= squared * (cosine * top - sine * bottom)
        curve = -2.0 * (sine * top + cosine * bottom)
        for k in range(3):
            value = phase_cot * coords[k] + slopes[k] + freqs[k] * curve
            high, low = split(value)
            back[k, rows, :] = high
            back[k, later, :] = low
        return carry

    lax.fori_loop(0, 4, sink, 0)
    for k in range(3):
        sums = nt_dot(ones, back[k, 0:128, :])
        put(("frequency", k), sums[0:1, 0:64] + sums[0:1, 64:128])


def lookup(matrix_rows, mask):
    return jnp.dot(matrix_rows, mask, precision=highest, preferred_element_type=f32)


def kernel(
    count,
    ff, fw, fb, fr, bf, bw, bb, br, wf, ww, wb, wr, table, field, cells, margins, source,
    gff, gfw, gfb, gfr, gbf, gbw, gbb, gbr, gwf, gww, gwb, gwr,
    flip, columns, lifted,
    waves_w, jets_w0, jets_w1, jets_w2, mix_w0, mix_w1,
    waves_b, jets_b0, jets_b1, jets_b2, mix_b0, mix_b1,
    waves_f, jets_f0, jets_f1, jets_f2, mix_f0, mix_f1,
    back, cots, back_f, cots_f,
    codes, halo_out, halo_in, small_out, small_in, parts, landed, reduced, gathered,
    halo_send, halo_recv, small_send, small_recv, rs_send, rs_recv, ag_send, ag_recv,
):
    me = lax.axis_index("gx")
    right, left = lax.rem(me + 1, count), lax.rem(me + count - 1, count)
    barrier = pltpu.get_barrier_semaphore()

    def greet(k, carry):
        pl.semaphore_signal(barrier, inc=1, device_id={"gx": lax.rem(me + k, count)})
        return carry

    lax.fori_loop(1, count, greet, 0)

    def halo_copy(phase, side):
        return pltpu.make_async_remote_copy(
            src_ref=halo_out.at[phase],
            dst_ref=halo_in.at[phase, side],
            send_sem=halo_send.at[phase, side],
            recv_sem=halo_recv.at[phase, side],
            device_id={"gx": right if side == 0 else left},
        )

    def spread(start_copy):
        def one(k, carry):
            start_copy(k, lax.rem(me + k, count))
            return carry

        lax.fori_loop(1, count, one, 0)

    def small_copy(k, peer):
        return pltpu.make_async_remote_copy(
            src_ref=small_out,
            dst_ref=small_in.at[k],
            send_sem=small_send.at[k],
            recv_sem=small_recv.at[k],
            device_id={"gx": peer},
        )

    def rs_copy(net, k, peer):
        return pltpu.make_async_remote_copy(
            src_ref=parts.at[net, peer],
            dst_ref=landed.at[net, k],
            send_sem=rs_send.at[net, k],
            recv_sem=rs_recv.at[net, k],
            device_id={"gx": peer},
        )

    def ag_copy(net, k, peer, owner):
        return pltpu.make_async_remote_copy(
            src_ref=reduced.at[net],
            dst_ref=gathered.at[net, owner],
            send_sem=ag_send.at[net, k],
            recv_sem=ag_recv.at[net, k],
            device_id={"gx": peer},
        )

    cell_row = cells[...]
    depth = lax.shift_right_logical(cell_row, 10)
    offset = me.astype(f32)
    along = offset + (depth.astype(f32) + 0.5) / GRID
    across = ((lax.shift_right_logical(cell_row, 5) & 31).astype(f32) + 0.5) / GRID
    upward = ((cell_row & 31).astype(f32) + 0.5) / GRID
    lane = lax.broadcasted_iota(jnp.int32, (1, 128), 1)
    codes[...] = jnp.full_like(codes, -1)
    codes[0:1, 0:32] = margins[0, 0:1, :]
    codes[0:1, 32:64] = margins[0, 1:2, :]
    mask = jnp.where(
        lax.broadcasted_iota(jnp.int32, (256, 128), 0) == codes[0:1, :], 1.0, 0.0
    ).astype(f32)
    zeros = jnp.zeros((5, 256), f32)
    halo_out[0] = lookup(jnp.concatenate([along, across, upward, zeros], axis=0), mask)

    pl.semaphore_wait(barrier, count - 1)
    for side in range(2):
        halo_copy(0, side).start()

    layer_pick = jnp.where(
        lax.broadcasted_iota(jnp.int32, (32, 256), 0) == depth, 1.0, 0.0
    ).astype(bf16)
    face = cell_row & 1023
    code_row = jnp.zeros((1, 256), f32)
    for chunk in range(8):
        layers = field[:, chunk * 128 : (chunk + 1) * 128].astype(f32).T.astype(bf16)
        picked = jnp.dot(layers, layer_pick, preferred_element_type=f32)
        here = lax.broadcasted_iota(jnp.int32, (128, 256), 0) + chunk * 128 == face
        code_row += jnp.sum(jnp.where(here, picked, 0.0), axis=0, keepdims=True)
    speeds = jnp.zeros((1, 256), f32)
    for level in range(table.shape[0]):
        speeds = jnp.where(code_row == float(level), table[level], speeds)
    slowness = 1.0 / (speeds * speeds)
    source_row = source[...]
    power_term = jnp.sum(source_row * source_row, axis=1, keepdims=True)

    points = (along, across, upward)
    lifted_w, lifted_f, lifted_b = lifted.at[0], lifted.at[1], lifted.at[2]
    columns_w, columns_f, columns_b = columns.at[0], columns.at[1], columns.at[2]
    whole_readout = wr[...].reshape(1, 128)
    prepare_net(flip, columns_w, lifted_w, wf[...], ww, wb[...], whole_readout)
    jets_w, mixes_w = (jets_w0, jets_w1, jets_w2), (mix_w0, mix_w1)
    whole_out = forward(columns_w, lifted_w, waves_w, jets_w, mixes_w, whole_readout, points, 256)

    prepare_net(flip, columns_f, lifted_f, ff[0], fw.at[0], fb[0], fr[...])
    for side in range(2):
        halo_copy(0, side).wait()
    guests = jnp.where(lane < 32, halo_in[0, 1], halo_in[0, 0])
    points_f = tuple(
        jnp.concatenate([points[k], guests[k : k + 1]], axis=1) for k in range(3)
    )
    jets_f, mixes_f = (jets_f0, jets_f1, jets_f2), (mix_f0, mix_f1)
    fine_out = forward(columns_f, lifted_f, waves_f, jets_f, mixes_f, fr[...], points_f, 384)
    wf_h, wf_s, wf_c = window_rows(points_f[0], offset, offset + 1.0)
    fine_value = wf_h * fine_out[0]
    fine_lap = wf_h * fine_out[2] + 2.0 * wf_s * fine_out[1] + wf_c * fine_out[0]
    zeros = jnp.zeros((6, 128), f32)
    halo_out[1] = jnp.concatenate([fine_value[:, 256:], fine_lap[:, 256:], zeros], axis=0)
    for side in range(2):
        halo_copy(1, side).start()

    prepare_net(flip, columns_b, lifted_b, bf[0], bw.at[0], bb[0], br[...])
    jets_b, mixes_b = (jets_b0, jets_b1, jets_b2), (mix_b0, mix_b1)
    block_out = forward(columns_b, lifted_b, waves_b, jets_b, mixes_b, br[...], points, 256)
    wb_h, wb_s, wb_c = window_rows(along, 0.0, float(BLOCK))
    value = fine_value[:, :256] + whole_out[0] + wb_h * block_out[0]
    laplace = (
        fine_lap[:, :256]
        + whole_out[2]
        + wb_h * block_out[2]
        + 2.0 * wb_s * block_out[1]
        + wb_c * block_out[0]
    )
    for side in range(2):
        halo_copy(1, side).wait()
    has_left = me > 0
    has_right = me < count - 1
    low_lane = (lane < 32) & has_left
    high_lane = (lane >= 32) & (lane < 64) & has_right
    extra = jnp.where(low_lane, halo_in[1, 0], jnp.where(high_lane, halo_in[1, 1], 0.0))
    extra = lax.dot_general(
        extra, mask, (((1,), (1,)), ((), ())), precision=highest, preferred_element_type=f32
    )
    value += extra[0:1]
    laplace += extra[1:2]
    residual = laplace / (kappa * kappa) + slowness * value - source_row
    value_cot = residual * slowness
    lap_cot = residual / (kappa * kappa)
    zeros = jnp.zeros((6, 256), f32)
    halo_out[2] = lookup(jnp.concatenate([value_cot, lap_cot, zeros], axis=0), mask)
    for side in range(2):
        halo_copy(2, side).start()

    share = 256 // count
    half = count // 2
    small_out[...] = jnp.zeros_like(small_out)
    small_out[14:15, :] = jnp.broadcast_to(power_term, (1, 128))

    def keep(net):
        def put(name, grad):
            if name == "readout":
                small_out[net * 6 + 5 : net * 6 + 6, :] = grad
            elif name[0] == "bias":
                small_out[net * 6 + 3 + name[1] : net * 6 + 4 + name[1], :] = grad
            elif name[0] == "frequency":
                small_out[net * 6 + name[1] : net * 6 + 1 + name[1], 0:64] = grad
            else:
                parts[net, name[1] * half : (name[1] + 1) * half] = grad.reshape(half, share, 128)

        return put

    backward(
        columns_w, lifted_w, waves_w, jets_w, mixes_w, back, cots, points,
        value_cot, jnp.zeros_like(value_cot), lap_cot, 256, keep(0),
    )
    spread(lambda k, peer: rs_copy(0, k, peer).start())
    backward(
        columns_b, lifted_b, waves_b, jets_b, mixes_b, back, cots, points,
        wb_h * value_cot + wb_c * lap_cot, 2.0 * wb_s * lap_cot, wb_h * lap_cot, 256, keep(1),
    )
    spread(lambda k, peer: rs_copy(1, k, peer).start())
    spread(lambda k, peer: small_copy(k, peer).start())

    def reduce(net):
        def arrive(k, total):
            rs_copy(net, k, lax.rem(me + k, count)).wait()
            return total + landed[net, k]

        total = lax.fori_loop(1, count, arrive, parts[net, me])
        reduced[net] = total
        gathered[net, me] = total
        spread(lambda k, peer: ag_copy(net, k, peer, me).start())

    for side in range(2):
        halo_copy(2, side).wait()
    low_lane = (lane < 32) & has_right
    high_lane = (lane >= 32) & (lane < 64) & has_left
    guest_cots = jnp.where(low_lane, halo_in[2, 1], jnp.where(high_lane, halo_in[2, 0], 0.0))
    value_f = jnp.concatenate([value_cot, guest_cots[0:1]], axis=1)
    lap_f = jnp.concatenate([lap_cot, guest_cots[1:2]], axis=1)

    def put_fine(name, grad):
        if name == "readout":
            gfr[...] = grad
        elif name[0] == "bias":
            gfb[0, name[1] : name[1] + 1, :] = grad
        elif name[0] == "frequency":
            gff[0, name[1] : name[1] + 1, :] = grad
        else:
            gfw[0, name[1]] = grad
            if name[1] == 1:
                reduce(0)
            else:
                reduce(1)

    backward(
        columns_f, lifted_f, waves_f, jets_f, mixes_f, back_f, cots_f, points_f,
        wf_h * value_f + wf_c * lap_f, 2.0 * wf_s * lap_f, wf_h * lap_f, 384, put_fine,
    )

    def add_small(k, total):
        small_copy(k, lax.rem(me + k, count)).wait()
        return total + small_in[k]

    small = lax.fori_loop(1, count, add_small, small_out[...])
    power = small[14:15, :] / (count * 256) + epsilon
    scale = 1.0 / (256 * power)
    narrow = scale[:, 0:64]
    gff[0] = gff[0] * narrow
    gfw[0] = gfw[0] * scale
    gfb[0] = gfb[0] * scale
    gfr[...] = gfr[...] * scale
    gwf[...] = small[0:3, 0:64] * narrow
    gwb[...] = small[3:5] * scale
    gwr[...] = (small[5:6] * scale).reshape(128)
    gbf[0] = small[6:9, 0:64] * narrow
    gbb[0] = small[9:11] * scale
    gbr[...] = small[11:12] * scale
    for net, target in ((0, gww), (1, gbw.at[0])):

        def settle(k, carry):
            owner = lax.rem(me + count - k, count)
            ag_copy(net, k, lax.rem(me + k, count), owner).wait()
            return carry

        lax.fori_loop(1, count, settle, 0)
        for layer in range(2):
            whole_part = gathered[net, layer * half : (layer + 1) * half].reshape(128, 128)
            target[layer] = whole_part * scale


def fused(*arrays):
    count = lax.axis_size("gx")
    vmem = pl.BlockSpec(memory_space=pltpu.VMEM)
    in_specs = [vmem] * len(arrays)
    in_specs[12] = pl.BlockSpec(memory_space=pltpu.SMEM)

    def net_scratch(width):
        return [
            pltpu.VMEM((2, 64, width), f32),
            pltpu.VMEM((5, 256, width), bf16),
            pltpu.VMEM((5, 256, width), bf16),
            pltpu.VMEM((3, 256, width), bf16),
            pltpu.VMEM((5, 128, width), f32),
            pltpu.VMEM((5, 128, width), f32),
        ]

    share = 256 // count
    dma = pltpu.SemaphoreType.DMA
    return pl.pallas_call(
        functools.partial(kernel, count),
        out_shape=[jax.ShapeDtypeStruct(a.shape, f32) for a in arrays[:12]],
        in_specs=in_specs,
        out_specs=[vmem] * 12,
        scratch_shapes=[
            pltpu.VMEM((128, 128), f32),
            pltpu.VMEM((3, 7, 128, 128), f32),
            pltpu.VMEM((3, 2, 2, 256, 256), bf16),
            *net_scratch(256),
            *net_scratch(256),
            *net_scratch(384),
            pltpu.VMEM((5, 256, 256), bf16),
            pltpu.VMEM((5, 128, 256), f32),
            pltpu.VMEM((5, 256, 384), bf16),
            pltpu.VMEM((5, 128, 384), f32),
            pltpu.VMEM((8, 128), jnp.int32),
            pltpu.VMEM((3, 8, 128), f32),
            pltpu.VMEM((3, 2, 8, 128), f32),
            pltpu.VMEM((16, 128), f32),
            pltpu.VMEM((count, 16, 128), f32),
            pltpu.VMEM((2, count, share, 128), f32),
            pltpu.VMEM((2, count, share, 128), f32),
            pltpu.VMEM((2, share, 128), f32),
            pltpu.VMEM((2, count, share, 128), f32),
            dma((3, 2)),
            dma((3, 2)),
            dma((count,)),
            dma((count,)),
            dma((2, count)),
            dma((2, count)),
            dma((2, count)),
            dma((2, count)),
        ],
        compiler_params=pltpu.CompilerParams(
            collective_id=0, has_side_effects=True, vmem_limit_bytes=48 * 1024 * 1024
        ),
        cost_estimate=pl.CostEstimate(
            flops=3_000_000_000, bytes_accessed=1_000_000, transcendentals=300_000
        ),
    )(*arrays)


def on_device(*arrays):
    one_block = arrays[4].shape[0] == 1
    return (fused if one_block else shards)(*arrays)


def solution(mesh):
    placed = (
        P(("groups", "gx"), None, None),
        P(("groups", "gx"), None, None, None),
        P(("groups", "gx"), None, None),
        P(("groups", "gx"), None),
        P("groups", None, None),
        P("groups", None, None, None),
        P("groups", None, None),
        P("groups", None),
        P("groups", None),
        P("groups", None, None),
        P("groups", None),
        P("groups"),
        P(),
        P(("groups", "gx"), None),
        P(("groups", "gx"), None),
        P(("groups", "gx"), None, None),
        P(("groups", "gx"), None),
    )
    return jax.shard_map(
        on_device,
        mesh=mesh,
        in_specs=placed,
        out_specs=(
            P(("groups", "gx"), None, None),
            P(("groups", "gx"), None, None, None),
            P(("groups", "gx"), None, None),
            P(("groups", "gx"), None),
            P("groups", None, None),
            P("groups", None, None, None),
            P("groups", None, None),
            P("groups", None),
            P("groups", None),
            P("groups", None, None),
            P("groups", None),
            P("groups"),
        ),
        check_vma=False,
    )
```

```python
import functools

import jax
import jax.numpy as jnp
from jax import lax
from jax.experimental import pallas as pl
from jax.experimental.pallas import tpu as pltpu
from jax.sharding import PartitionSpec as P

GRID = 32
STRIP = 4
BLOCK = 16


kappa = 3.125
epsilon = 1e-06
highest = lax.Precision.HIGHEST


def with_halo(cells, sides, width):
    for axis, dim in sides:
        count = lax.axis_size(axis)
        ends = count - 1
        head = lax.slice_in_dim(cells, 0, width, axis=dim)
        tail = lax.slice_in_dim(cells, cells.shape[dim] - width, cells.shape[dim], axis=dim)
        cells = jnp.concatenate(
            [
                lax.ppermute(tail, axis, [(i, (i + 1) % count) for i in range(ends)]),
                cells,
                lax.ppermute(head, axis, [((i + 1) % count, i) for i in range(ends)]),
            ],
            axis=dim,
        )
    return cells


def network(params, points):
    frequency, weights, biases, readout = params
    unit_count = readout.shape[0]
    point_count = points.shape[0]
    phases = jnp.dot(points, frequency, precision=highest, preferred_element_type=jnp.float32)
    sines = jnp.sin(phases)
    cosines = jnp.cos(phases)
    squared = jnp.sum(frequency * frequency, axis=0)
    channels = [jnp.concatenate([sines, cosines], axis=1)]
    for axis_pick in range(3):
        channels.append(
            jnp.concatenate([cosines * frequency[axis_pick], -sines * frequency[axis_pick]], axis=1)
        )
    channels.append(jnp.concatenate([-sines * squared, -cosines * squared], axis=1))
    jets = jnp.stack(channels)
    for section_index in range(weights.shape[0]):
        mixture = jnp.dot(
            jets.reshape(-1, unit_count),
            weights[section_index],
            precision=highest,
            preferred_element_type=jnp.float32,
        ).reshape(5, point_count, unit_count)
        active = jnp.tanh(mixture[0] + biases[section_index])
        derivative = 1.0 - active * active
        second = -2.0 * active * derivative
        gradients = derivative * mixture[1:4]
        curvature = derivative * mixture[4] + second * jnp.sum(mixture[1:4] * mixture[1:4], axis=0)
        jets = jnp.concatenate([active[None], gradients, curvature[None]], axis=0)
    output = jnp.dot(
        jets.reshape(-1, unit_count), readout, precision=highest, preferred_element_type=jnp.float32
    ).reshape(5, point_count)
    return (output[0], output[1], output[4])


def smooth_ramp(position):
    inside = (position > 0.0) & (position < 1.0)
    clipped = jnp.clip(position, 0.0, 1.0)
    height = 0.5 - 0.5 * jnp.cos(jnp.pi * clipped)
    slopes = jnp.where(inside, 0.5 * jnp.pi * jnp.sin(jnp.pi * clipped), 0.0)
    curvature = jnp.where(inside, 0.5 * jnp.pi * jnp.pi * jnp.cos(jnp.pi * clipped), 0.0)
    return (height, slopes, curvature)


def window(abscissa, lower_edge, upper_edge, margin):
    inverse_width = 0.5 / margin
    rise_height, rise_slope, rise_curve = smooth_ramp(
        (abscissa - lower_edge + margin) * inverse_width
    )
    fall_height, fall_slope, fall_curve = smooth_ramp(
        (upper_edge + margin - abscissa) * inverse_width
    )
    height = rise_height * fall_height
    slopes = inverse_width * (rise_slope * fall_height - rise_height * fall_slope)
    curvature = (
        inverse_width
        * inverse_width
        * (rise_curve * fall_height - 2.0 * rise_slope * fall_slope + rise_height * fall_curve)
    )
    return (height, slopes, curvature)


def windowed(params, points, lower_edge, upper_edge, margin):
    net_value, along_first, net_laplace = network(params, points)
    height, slopes, curvature = window(points[:, 0], lower_edge, upper_edge, margin)
    return (
        height * net_value,
        height * net_laplace + 2.0 * slopes * along_first + curvature * net_value,
    )


def locate(cell_ids, offset):
    depth_index = (cell_ids // (GRID * GRID)).astype(jnp.float32)
    row_index = (cell_ids // GRID % GRID).astype(jnp.float32)
    column = (cell_ids % GRID).astype(jnp.float32)
    return jnp.stack(
        [offset + (depth_index + 0.5) / GRID, (row_index + 0.5) / GRID, (column + 0.5) / GRID],
        axis=1,
    )


def select_row(params, which):
    return jax.tree.map(lambda array: array[which], params)


def shards(
    fine_frequency,
    fine_weights,
    fine_biases,
    fine_readout,
    block_frequency,
    block_weights,
    block_biases,
    block_readout,
    whole_frequency,
    whole_weights,
    whole_biases,
    whole_readout,
    speed_table,
    speed_field,
    point_cells,
    margin_points,
    source,
):
    margin = STRIP / GRID
    device_index = lax.axis_index("gx")
    device_count = lax.axis_size("gx")
    offset = device_index.astype(jnp.float32)
    fine_own = (fine_frequency[0], fine_weights[0], fine_biases[0], fine_readout[0])
    block = (block_frequency, block_weights, block_biases, block_readout)
    whole = (whole_frequency, whole_weights, whole_biases, whole_readout)
    local_source = source[0]
    point_total = local_source.shape[0]
    strip_count = margin_points.shape[2]
    power_term = jnp.sum(local_source * local_source)
    power_total = lax.psum(power_term, "gx")
    cell_ids = point_cells[0]
    points = locate(cell_ids, offset)
    speed_codes = speed_field.reshape(-1)[cell_ids]
    table_levels = jnp.arange(speed_table.shape[0], dtype=jnp.int32)
    speeds = jnp.sum(
        jnp.where(speed_codes[:, None] == table_levels[None, :], speed_table[None, :], 0.0), axis=1
    )
    slowness = 1.0 / (speeds * speeds)
    left_ids = margin_points[0, 0]
    right_ids = margin_points[0, 1]
    left_points = points[left_ids]
    right_points = points[right_ids]
    home = device_index // BLOCK
    left_block = jnp.maximum(device_index - 1, 0) // BLOCK
    right_block = jnp.minimum(device_index + 1, device_count - 1) // BLOCK
    left_edge = ((device_index % BLOCK == 0) & (device_index > 0)).astype(jnp.float32)
    right_edge = ((device_index % BLOCK == BLOCK - 1) & (device_index < device_count - 1)).astype(
        jnp.float32
    )

    def shared_terms(fine_params, block_params, whole_params):
        own_value, own_laplace = windowed(fine_params, points, offset, offset + 1.0, margin)
        home_floor = (home * BLOCK).astype(jnp.float32)
        home_value, home_laplace = windowed(
            select_row(block_params, home), points, home_floor, home_floor + BLOCK, margin
        )
        left_floor = (left_block * BLOCK).astype(jnp.float32)
        lower_value, lower_laplace = windowed(
            select_row(block_params, left_block),
            left_points,
            left_floor,
            left_floor + BLOCK,
            margin,
        )
        right_floor = (right_block * BLOCK).astype(jnp.float32)
        upper_value, upper_laplace = windowed(
            select_row(block_params, right_block),
            right_points,
            right_floor,
            right_floor + BLOCK,
            margin,
        )
        whole_value, whole_along, whole_laplace = network(whole_params, points)
        return (
            own_value + home_value + whole_value,
            own_laplace + home_laplace + whole_laplace,
            left_edge * jnp.stack([lower_value, lower_laplace]),
            right_edge * jnp.stack([upper_value, upper_laplace]),
        )

    strip_coords = jnp.concatenate([left_points, right_points], axis=0).T
    padded = with_halo(strip_coords, (("gx", 1),), strip_count)
    guest_points = jnp.concatenate([padded[:, :strip_count], padded[:, -strip_count:]], axis=1).T

    def guest_terms(fine_params):
        guest_value, guest_laplace = windowed(
            fine_params, guest_points, offset, offset + 1.0, margin
        )
        return jnp.stack([guest_value, guest_laplace])

    guest_parts, guest_pull = jax.vjp(guest_terms, fine_own)
    arrived = with_halo(guest_parts, (("gx", 1),), strip_count)
    from_left = arrived[:, :strip_count]
    from_right = arrived[:, -strip_count:]
    (field_value, field_laplace, left_extra, right_extra), shared_pull = jax.vjp(
        shared_terms, fine_own, block, whole
    )
    left_total = left_extra + from_left
    right_total = right_extra + from_right
    field_value = field_value.at[left_ids].add(left_total[0]).at[right_ids].add(right_total[0])
    field_laplace = field_laplace.at[left_ids].add(left_total[1]).at[right_ids].add(right_total[1])
    residual = field_laplace / (kappa * kappa) + slowness * field_value - local_source
    value_weight = residual * slowness
    laplace_weight = residual / (kappa * kappa)
    left_cot = jnp.stack([value_weight[left_ids], laplace_weight[left_ids]])
    right_cot = jnp.stack([value_weight[right_ids], laplace_weight[right_ids]])
    fine_grad, block_grad, whole_grad = shared_pull(
        (value_weight, laplace_weight, left_cot, right_cot)
    )
    sent_back = jnp.concatenate([left_cot, right_cot], axis=1)
    returned = with_halo(sent_back, (("gx", 1),), strip_count)
    guest_cot = jnp.concatenate([returned[:, :strip_count], returned[:, -strip_count:]], axis=1)
    extra_grad = guest_pull(guest_cot)[0]
    fine_grad = jax.tree.map(
        lambda first_part, second_part: first_part + second_part, fine_grad, extra_grad
    )
    whole_sum = lax.psum((whole_grad[0], whole_grad[1], whole_grad[2], whole_grad[3]), "gx")
    block_sum = lax.psum((block_grad[0], block_grad[1], block_grad[2], block_grad[3]), "gx")
    power = power_total / (device_count * point_total) + epsilon
    scale = 1.0 / (point_total * power)
    return (
        fine_grad[0][None] * scale,
        fine_grad[1][None] * scale,
        fine_grad[2][None] * scale,
        fine_grad[3][None] * scale,
        block_sum[0] * scale,
        block_sum[1] * scale,
        block_sum[2] * scale,
        block_sum[3] * scale,
        whole_sum[0] * scale,
        whole_sum[1] * scale,
        whole_sum[2] * scale,
        whole_sum[3] * scale,
    )


BLK_ROWS = 16
f32 = jnp.float32
bf16 = jnp.bfloat16


def split(values):
    high = values.astype(bf16)
    return high, (values - high.astype(f32)).astype(bf16)


def nt_dot(first, second):
    return lax.dot_general(first, second, (((1,), (1,)), ((), ())), preferred_element_type=f32)


def sincos(angle):
    turns = jnp.floor(angle * 0.6366197723675814 + 0.5)
    quadrant = turns.astype(jnp.int32)
    rest = angle - turns * 1.5703125
    rest = rest - turns * 4.837512969970703125e-4
    rest = rest - turns * 7.54978995489188216e-8
    square = rest * rest
    sine = (-1.9515295891e-4 * square + 8.3321608736e-3) * square - 1.6666654611e-1
    sine = rest + rest * square * sine
    cosine = (2.443315711809948e-5 * square - 1.388731625493765e-3) * square + 4.166664568298827e-2
    cosine = 1.0 - 0.5 * square + square * square * cosine
    odd = (quadrant & 1) == 1
    first = jnp.where(odd, cosine, sine)
    second = jnp.where(odd, sine, cosine)
    first = jnp.where((quadrant & 2) == 2, -first, first)
    second = jnp.where(((quadrant + 1) & 2) == 2, -second, second)
    return first, second


def ramp_rows(position):
    inside = (position > 0.0) & (position < 1.0)
    sine, cosine = sincos(jnp.pi * jnp.clip(position, 0.0, 1.0))
    return (
        0.5 - 0.5 * cosine,
        jnp.where(inside, 0.5 * jnp.pi * sine, 0.0),
        jnp.where(inside, 0.5 * jnp.pi * jnp.pi * cosine, 0.0),
    )


def window_rows(abscissa, lower_edge, upper_edge):
    margin = STRIP / GRID
    inverse_width = 0.5 / margin
    rise, rise_slope, rise_curve = ramp_rows((abscissa - lower_edge + margin) * inverse_width)
    fall, fall_slope, fall_curve = ramp_rows((upper_edge + margin - abscissa) * inverse_width)
    return (
        rise * fall,
        inverse_width * (rise_slope * fall - rise * fall_slope),
        inverse_width
        * inverse_width
        * (rise_curve * fall - 2.0 * rise_slope * fall_slope + rise * fall_curve),
    )


def wide(column, width):
    return jnp.concatenate([column] * (width // 128), axis=1)


def stacked_row(row):
    high, low = split(row)
    high = high.astype(f32)
    low = low.astype(f32)
    top = jnp.concatenate([high, high], axis=1)
    bottom = jnp.concatenate([low, jnp.zeros_like(low)], axis=1)
    level = lax.broadcasted_iota(jnp.int32, (16, top.shape[1]), 0)
    return jnp.where(level == 0, top, jnp.where(level == 1, bottom, 0.0)).astype(bf16)


def two_rows(row):
    high, low = split(row)
    level = lax.broadcasted_iota(jnp.int32, (16, row.shape[1]), 0)
    return jnp.where(
        level == 0, high.astype(f32), jnp.where(level == 1, low.astype(f32), 0.0)
    ).astype(bf16)


def rows_at(step):
    return pl.ds(pl.multiple_of(step * BLK_ROWS, BLK_ROWS), BLK_ROWS)


def low_rows_at(step, start):
    return pl.ds(pl.multiple_of(step * BLK_ROWS + start, BLK_ROWS), BLK_ROWS)


def prepare_net(flip, columns, lifted, frequency, weights, biases, readout):
    flip[...] = jnp.zeros_like(flip)
    flip[0:2, :] = biases
    flip[2:3, :] = readout
    flip[3:6, 0:64] = frequency
    flip[3:6, 64:128] = frequency
    turned = flip[...].T
    parts = [jnp.broadcast_to(turned[:, k : k + 1], (128, 128)) for k in range(6)]
    for k in range(6):
        columns[k] = parts[k]
    columns[6] = parts[3] * parts[3] + parts[4] * parts[4] + parts[5] * parts[5]
    for layer in range(2):
        for which in range(2):
            matrix = weights[layer]
            high, low = split(matrix.T if which == 0 else matrix)
            lifted[layer, which, 0:128, 0:128] = high
            lifted[layer, which, 0:128, 128:256] = high
            lifted[layer, which, 128:256, 0:128] = low
            lifted[layer, which, 128:256, 128:256] = jnp.zeros_like(low)


def apply_lifted(matrix, stacked, result):
    for channel in range(5):
        product = jnp.dot(matrix, stacked[channel], preferred_element_type=f32)
        result[channel] = product[0:128] + product[128:256]


def store_split(target, channel, step, value, start=0):
    high, low = split(value)
    target[channel, low_rows_at(step, start), :] = high
    target[channel, low_rows_at(step, start + 128), :] = low


def forward(columns, lifted, waves, jets, mixes, readout, coords, width):
    along, across, upward = coords

    def lift(step, carry):
        rows = rows_at(step)
        freqs = [wide(columns[3 + k, rows, :], width) for k in range(3)]
        squared = wide(columns[6, rows, :], width)
        phase = along * freqs[0] + across * freqs[1] + upward * freqs[2]
        sine, cosine = sincos(phase)
        waves[0, rows, :] = sine
        waves[1, rows, :] = cosine
        store_split(jets[0], 0, step, sine)
        store_split(jets[0], 0, step, cosine, 64)
        for k in range(3):
            store_split(jets[0], 1 + k, step, cosine * freqs[k])
            store_split(jets[0], 1 + k, step, -sine * freqs[k], 64)
        store_split(jets[0], 4, step, -sine * squared)
        store_split(jets[0], 4, step, -cosine * squared, 64)
        return carry

    lax.fori_loop(0, 4, lift, 0)
    for layer in range(2):
        mix = mixes[layer]
        target = jets[layer + 1]
        apply_lifted(lifted[layer, 0], jets[layer], mix)

        def activate(step, carry):
            rows = rows_at(step)
            active = jnp.tanh(mix[0, rows, :] + wide(columns[layer, rows, :], width))
            derivative = 1.0 - active * active
            second = -2.0 * active * derivative
            m1, m2, m3, m4 = [mix[k, rows, :] for k in range(1, 5)]
            mix[0, rows, :] = active
            curvature = derivative * m4 + second * (m1 * m1 + m2 * m2 + m3 * m3)
            store_split(target, 0, step, active)
            store_split(target, 1, step, derivative * m1)
            if layer == 0:
                store_split(target, 2, step, derivative * m2)
                store_split(target, 3, step, derivative * m3)
                store_split(target, 4, step, curvature)
            else:
                store_split(target, 2, step, curvature)
            return carry

        lax.fori_loop(0, 8, activate, 0)
    left = stacked_row(readout)
    outs = []
    for channel in range(3):
        product = jnp.dot(left, jets[2][channel], preferred_element_type=f32)
        outs.append(product[0:1] + product[1:2])
    return outs


def backward(columns, lifted, waves, jets, mixes, back, cots, coords, alpha, beta, gamma, width, put):
    readout_rows = jnp.zeros((16, 256), f32)
    for channel, row in enumerate((alpha, beta, gamma)):
        readout_rows += nt_dot(two_rows(row), jets[2][channel])
    readout_rows = readout_rows[0:1] + readout_rows[1:2]
    put("readout", readout_rows[:, 0:128] + readout_rows[:, 128:256])
    ones = jnp.ones((16, width), bf16)
    for layer in (1, 0):
        mix = mixes[layer]

        def pull(step, carry):
            rows = rows_at(step)
            active = mix[0, rows, :]
            derivative = 1.0 - active * active
            second = -2.0 * active * derivative
            m = [mix[k, rows, :] for k in range(1, 5)]
            square = m[0] * m[0] + m[1] * m[1] + m[2] * m[2]
            if layer == 1:
                weight = wide(columns[2, rows, :], width)
                active_cot, curve_cot = weight * alpha, weight * gamma
                slope_cots = [weight * beta, None, None]
            else:
                active_cot, curve_cot = cots[0, rows, :], cots[4, rows, :]
                slope_cots = [cots[k, rows, :] for k in range(1, 4)]
            derivative_cot = curve_cot * m[3]
            for k in range(3):
                if slope_cots[k] is not None:
                    derivative_cot += slope_cots[k] * m[k]
            second_cot = curve_cot * square
            double = 2.0 * curve_cot * second
            store_split(back, 4, step, curve_cot * derivative)
            for k in range(3):
                value = double * m[k]
                if slope_cots[k] is not None:
                    value += slope_cots[k] * derivative
                store_split(back, 1 + k, step, value)
            derivative_cot = derivative_cot - 2.0 * active * second_cot
            active_cot = active_cot - 2.0 * (derivative * second_cot + active * derivative_cot)
            store_split(back, 0, step, active_cot * derivative)
            return carry

        lax.fori_loop(0, 8, pull, 0)
        bias_rows = nt_dot(ones, back[0])
        put(("bias", layer), bias_rows[0:1, 0:128] + bias_rows[0:1, 128:256])
        grad = jnp.zeros((256, 256), f32)
        for channel in range(5):
            grad += nt_dot(jets[layer][channel], back[channel])
        grad = grad[0:128] + grad[128:256]
        put(("weight", layer), grad[:, 0:128] + grad[:, 128:256])
        apply_lifted(lifted[layer, 1], back, cots)

    def sink(step, carry):
        rows = rows_at(step)
        later = low_rows_at(step, 64)
        sine, cosine = waves[0, rows, :], waves[1, rows, :]
        squared = wide(columns[6, rows, :], width)
        freqs = [wide(columns[3 + k, rows, :], width) for k in range(3)]
        phase_cot = cosine * cots[0, rows, :] - sine * cots[0, later, :]
        slopes = []
        for k in range(3):
            top, bottom = cots[1 + k, rows, :], cots[1 + k, later, :]
            phase_cot -= freqs[k] * (sine * top + cosine * bottom)
            slopes.append(cosine * top - sine * bottom)
        top, bottom = cots[4, rows, :], cots[4, later, :]
        phase_cot -= squared * (cosine * top - sine * bottom)
        curve = -2.0 * (sine * top + cosine * bottom)
        for k in range(3):
            value = phase_cot * coords[k] + slopes[k] + freqs[k] * curve
            high, low = split(value)
            back[k, rows, :] = high
            back[k, later, :] = low
        return carry

    lax.fori_loop(0, 4, sink, 0)
    for k in range(3):
        sums = nt_dot(ones, back[k, 0:128, :])
        put(("frequency", k), sums[0:1, 0:64] + sums[0:1, 64:128])


def lookup(matrix_rows, mask):
    return jnp.dot(matrix_rows, mask, precision=highest, preferred_element_type=f32)


def kernel(
    count,
    ff_h, fw_h, fb_h, fr_h, bf_h, bw_h, bb_h, br_h, wf_h, ww_h, wb_h, wr_h,
    table_h, field_h, cells_h, margins_h, source_h,
    gff, gfw, gfb, gfr, gbf, gbw, gbb, gbr, gwf, gww, gwb, gwr,
    ff, fw, fb, fr, bf, bw, bb, br, wf, ww, wb, wr, table, field, cells, margins, source,
    load_sem, fine_out_w, fine_out_s,
    flip, columns, lifted,
    waves_w, jets_w0, jets_w1, jets_w2, mix_w0, mix_w1,
    waves_b, jets_b0, jets_b1, jets_b2, mix_b0, mix_b1,
    waves_f, jets_f0, jets_f1, jets_f2, mix_f0, mix_f1,
    back, cots, back_f, cots_f,
    codes, halo_out, halo_in, small_out, small_in, parts, landed, reduced, gathered,
    halo_send, halo_recv, small_send, small_recv, rs_send, rs_recv, ag_send, ag_recv,
):
    me = lax.axis_index("gx")
    right, left = lax.rem(me + 1, count), lax.rem(me + count - 1, count)
    barrier = pltpu.get_barrier_semaphore()
    operands = (
        (cells_h, cells), (margins_h, margins), (field_h, field), (table_h, table),
        (wf_h, wf), (wb_h, wb), (wr_h, wr), (ww_h, ww), (source_h, source),
        (ff_h, ff), (fb_h, fb), (fr_h, fr), (fw_h, fw),
        (bf_h, bf), (bb_h, bb), (br_h, br), (bw_h, bw),
    )
    loads = [
        pltpu.make_async_copy(far, near, load_sem.at[k]) for k, (far, near) in enumerate(operands)
    ]

    def greet(k, carry):
        pl.semaphore_signal(barrier, inc=1, device_id={"gx": lax.rem(me + k, count)})
        return carry

    lax.fori_loop(1, count, greet, 0)
    for load in loads:
        load.start()

    def halo_copy(phase, side):
        return pltpu.make_async_remote_copy(
            src_ref=halo_out.at[phase],
            dst_ref=halo_in.at[phase, side],
            send_sem=halo_send.at[phase, side],
            recv_sem=halo_recv.at[phase, side],
            device_id={"gx": right if side == 0 else left},
        )

    def spread(start_copy):
        def one(k, carry):
            start_copy(k, lax.rem(me + k, count))
            return carry

        lax.fori_loop(1, count, one, 0)

    def small_copy(k, peer):
        return pltpu.make_async_remote_copy(
            src_ref=small_out,
            dst_ref=small_in.at[k],
            send_sem=small_send.at[k],
            recv_sem=small_recv.at[k],
            device_id={"gx": peer},
        )

    def rs_copy(net, k, peer):
        return pltpu.make_async_remote_copy(
            src_ref=parts.at[net, peer],
            dst_ref=landed.at[net, k],
            send_sem=rs_send.at[net, k],
            recv_sem=rs_recv.at[net, k],
            device_id={"gx": peer},
        )

    def ag_copy(net, k, peer, owner):
        return pltpu.make_async_remote_copy(
            src_ref=reduced.at[net],
            dst_ref=gathered.at[net, owner],
            send_sem=ag_send.at[net, k],
            recv_sem=ag_recv.at[net, k],
            device_id={"gx": peer},
        )

    for load in loads[0:2]:
        load.wait()
    cell_row = cells[...]
    depth = lax.shift_right_logical(cell_row, 10)
    offset = me.astype(f32)
    along = offset + (depth.astype(f32) + 0.5) / GRID
    across = ((lax.shift_right_logical(cell_row, 5) & 31).astype(f32) + 0.5) / GRID
    upward = ((cell_row & 31).astype(f32) + 0.5) / GRID
    lane = lax.broadcasted_iota(jnp.int32, (1, 128), 1)
    codes[...] = jnp.full_like(codes, -1)
    codes[0:1, 0:32] = margins[0, 0:1, :]
    codes[0:1, 32:64] = margins[0, 1:2, :]
    mask = jnp.where(
        lax.broadcasted_iota(jnp.int32, (256, 128), 0) == codes[0:1, :], 1.0, 0.0
    ).astype(f32)
    zeros = jnp.zeros((5, 256), f32)
    halo_out[0] = lookup(jnp.concatenate([along, across, upward, zeros], axis=0), mask)

    pl.semaphore_wait(barrier, count - 1)
    for side in range(2):
        halo_copy(0, side).start()

    for load in loads[2:9]:
        load.wait()
    layer_pick = jnp.where(
        lax.broadcasted_iota(jnp.int32, (32, 256), 0) == depth, 1.0, 0.0
    ).astype(bf16)
    face = cell_row & 1023
    code_row = jnp.zeros((1, 256), f32)
    for chunk in range(8):
        layers = field[:, chunk * 128 : (chunk + 1) * 128].astype(f32).T.astype(bf16)
        picked = jnp.dot(layers, layer_pick, preferred_element_type=f32)
        here = lax.broadcasted_iota(jnp.int32, (128, 256), 0) + chunk * 128 == face
        code_row += jnp.sum(jnp.where(here, picked, 0.0), axis=0, keepdims=True)
    speeds = jnp.zeros((1, 256), f32)
    for level in range(table.shape[0]):
        speeds = jnp.where(code_row == float(level), table[level], speeds)
    slowness = 1.0 / (speeds * speeds)
    source_row = source[...]
    power_term = jnp.sum(source_row * source_row, axis=1, keepdims=True)

    points = (along, across, upward)
    lifted_w, lifted_f, lifted_b = lifted.at[0], lifted.at[1], lifted.at[2]
    columns_w, columns_f, columns_b = columns.at[0], columns.at[1], columns.at[2]
    whole_readout = wr[...].reshape(1, 128)
    prepare_net(flip, columns_w, lifted_w, wf[...], ww, wb[...], whole_readout)
    jets_w, mixes_w = (jets_w0, jets_w1, jets_w2), (mix_w0, mix_w1)
    whole_out = forward(columns_w, lifted_w, waves_w, jets_w, mixes_w, whole_readout, points, 256)

    for load in loads[9:13]:
        load.wait()
    prepare_net(flip, columns_f, lifted_f, ff[...].reshape(3, 64), fw.at[0], fb[0], fr[...])
    for side in range(2):
        halo_copy(0, side).wait()
    guests = jnp.where(lane < 32, halo_in[0, 1], halo_in[0, 0])
    points_f = tuple(
        jnp.concatenate([points[k], guests[k : k + 1]], axis=1) for k in range(3)
    )
    jets_f, mixes_f = (jets_f0, jets_f1, jets_f2), (mix_f0, mix_f1)
    fine_out = forward(columns_f, lifted_f, waves_f, jets_f, mixes_f, fr[...], points_f, 384)
    own_h, own_s, own_c = window_rows(points_f[0], offset, offset + 1.0)
    fine_value = own_h * fine_out[0]
    fine_lap = own_h * fine_out[2] + 2.0 * own_s * fine_out[1] + own_c * fine_out[0]
    zeros = jnp.zeros((6, 128), f32)
    halo_out[1] = jnp.concatenate([fine_value[:, 256:], fine_lap[:, 256:], zeros], axis=0)
    for side in range(2):
        halo_copy(1, side).start()

    for load in loads[13:17]:
        load.wait()
    prepare_net(flip, columns_b, lifted_b, bf[...].reshape(3, 64), bw.at[0], bb[0], br[...])
    jets_b, mixes_b = (jets_b0, jets_b1, jets_b2), (mix_b0, mix_b1)
    block_out = forward(columns_b, lifted_b, waves_b, jets_b, mixes_b, br[...], points, 256)
    home_h, home_s, home_c = window_rows(along, 0.0, float(BLOCK))
    value = fine_value[:, :256] + whole_out[0] + home_h * block_out[0]
    laplace = (
        fine_lap[:, :256]
        + whole_out[2]
        + home_h * block_out[2]
        + 2.0 * home_s * block_out[1]
        + home_c * block_out[0]
    )
    for side in range(2):
        halo_copy(1, side).wait()
    has_left = me > 0
    has_right = me < count - 1
    low_lane = (lane < 32) & has_left
    high_lane = (lane >= 32) & (lane < 64) & has_right
    extra = jnp.where(low_lane, halo_in[1, 0], jnp.where(high_lane, halo_in[1, 1], 0.0))
    extra = lax.dot_general(
        extra, mask, (((1,), (1,)), ((), ())), precision=highest, preferred_element_type=f32
    )
    value += extra[0:1]
    laplace += extra[1:2]
    residual = laplace / (kappa * kappa) + slowness * value - source_row
    value_cot = residual * slowness
    lap_cot = residual / (kappa * kappa)
    zeros = jnp.zeros((6, 256), f32)
    halo_out[2] = lookup(jnp.concatenate([value_cot, lap_cot, zeros], axis=0), mask)
    for side in range(2):
        halo_copy(2, side).start()

    share = 256 // count
    half = count // 2
    small_out[...] = jnp.zeros_like(small_out)
    small_out[14:15, :] = jnp.broadcast_to(power_term, (1, 128))

    def keep(net):
        def put(name, grad):
            if name == "readout":
                small_out[net * 6 + 5 : net * 6 + 6, :] = grad
            elif name[0] == "bias":
                small_out[net * 6 + 3 + name[1] : net * 6 + 4 + name[1], :] = grad
            elif name[0] == "frequency":
                small_out[net * 6 + name[1] : net * 6 + 1 + name[1], 0:64] = grad
            else:
                parts[net, name[1] * half : (name[1] + 1) * half] = grad.reshape(half, share, 128)

        return put

    backward(
        columns_w, lifted_w, waves_w, jets_w, mixes_w, back, cots, points,
        value_cot, jnp.zeros_like(value_cot), lap_cot, 256, keep(0),
    )
    spread(lambda k, peer: rs_copy(0, k, peer).start())
    backward(
        columns_b, lifted_b, waves_b, jets_b, mixes_b, back, cots, points,
        home_h * value_cot + home_c * lap_cot, 2.0 * home_s * lap_cot, home_h * lap_cot, 256, keep(1),
    )
    spread(lambda k, peer: rs_copy(1, k, peer).start())
    spread(lambda k, peer: small_copy(k, peer).start())

    def reduce(net):
        def arrive(k, total):
            rs_copy(net, k, lax.rem(me + k, count)).wait()
            return total + landed[net, k]

        total = lax.fori_loop(1, count, arrive, parts[net, me])
        reduced[net] = total
        gathered[net, me] = total
        spread(lambda k, peer: ag_copy(net, k, peer, me).start())

    for side in range(2):
        halo_copy(2, side).wait()
    low_lane = (lane < 32) & has_right
    high_lane = (lane >= 32) & (lane < 64) & has_left
    guest_cots = jnp.where(low_lane, halo_in[2, 1], jnp.where(high_lane, halo_in[2, 0], 0.0))
    value_f = jnp.concatenate([value_cot, guest_cots[0:1]], axis=1)
    lap_f = jnp.concatenate([lap_cot, guest_cots[1:2]], axis=1)

    fine_out_s[...] = jnp.zeros_like(fine_out_s)

    def put_fine(name, grad):
        if name == "readout":
            fine_out_s[5:6, :] = grad
        elif name[0] == "bias":
            fine_out_s[3 + name[1] : 4 + name[1], :] = grad
        elif name[0] == "frequency":
            fine_out_s[name[1] : name[1] + 1, 0:64] = grad
        else:
            fine_out_w[name[1]] = grad
            if name[1] == 1:
                reduce(0)
            else:
                reduce(1)

    backward(
        columns_f, lifted_f, waves_f, jets_f, mixes_f, back_f, cots_f, points_f,
        own_h * value_f + own_c * lap_f, 2.0 * own_s * lap_f, own_h * lap_f, 384, put_fine,
    )

    def add_small(k, total):
        small_copy(k, lax.rem(me + k, count)).wait()
        return total + small_in[k]

    small = lax.fori_loop(1, count, add_small, small_out[...])
    power = small[14:15, :] / (count * 256) + epsilon
    scale = 1.0 / (256 * power)
    narrow = scale[:, 0:64]
    gff[...] = (fine_out_s[0:3, 0:64] * narrow).reshape(3, 1, 64)
    gfw[0] = fine_out_w[...] * scale
    gfb[0] = fine_out_s[3:5, :] * scale
    gfr[...] = fine_out_s[5:6, :] * scale
    gwf[...] = small[0:3, 0:64] * narrow
    gwb[...] = small[3:5] * scale
    gwr[...] = (small[5:6] * scale).reshape(128)
    gbf[...] = (small[6:9, 0:64] * narrow).reshape(3, 1, 64)
    gbb[0] = small[9:11] * scale
    gbr[...] = small[11:12] * scale
    for net, target in ((0, gww), (1, gbw.at[0])):

        def settle(k, carry):
            owner = lax.rem(me + count - k, count)
            ag_copy(net, k, lax.rem(me + k, count), owner).wait()
            return carry

        lax.fori_loop(1, count, settle, 0)
        for layer in range(2):
            part = gathered[net, layer * half : (layer + 1) * half]
            target[layer] = part.reshape(128, 128) * scale


def finish(*refs):
    size = (len(refs) - 2) // 3
    given, wanted, held = refs[:size], refs[size : 2 * size], refs[2 * size : 3 * size]
    loads = [pltpu.make_async_copy(given[k], held[k], refs[-2].at[k]) for k in range(size)]
    stores = [pltpu.make_async_copy(held[k], wanted[k], refs[-1].at[k]) for k in range(size)]
    for load in loads:
        load.start()
    for load, store in zip(loads, stores):
        load.wait()
        store.start()
    for store in stores:
        store.wait()


def fused(*arrays):
    count = lax.axis_size("gx")
    vmem = pl.BlockSpec(memory_space=pltpu.VMEM)
    far = pl.BlockSpec(memory_space=pltpu.HBM)
    arrays = list(arrays)
    for k in (0, 4):
        arrays[k] = arrays[k].transpose(1, 0, 2)
    near = [pltpu.VMEM(a.shape, a.dtype) for a in arrays]
    near[12] = pltpu.SMEM(arrays[12].shape, f32)

    def net_scratch(width):
        return [
            pltpu.VMEM((2, 64, width), f32),
            pltpu.VMEM((5, 256, width), bf16),
            pltpu.VMEM((5, 256, width), bf16),
            pltpu.VMEM((3, 256, width), bf16),
            pltpu.VMEM((5, 128, width), f32),
            pltpu.VMEM((5, 128, width), f32),
        ]

    share = 256 // count
    dma = pltpu.SemaphoreType.DMA
    results = pl.pallas_call(
        functools.partial(kernel, count),
        out_shape=[jax.ShapeDtypeStruct(a.shape, f32) for a in arrays[:12]],
        in_specs=[far] * 17,
        out_specs=[vmem] * 12,
        scratch_shapes=[
            *near,
            dma((17,)),
            pltpu.VMEM((2, 128, 128), f32),
            pltpu.VMEM((8, 128), f32),
            pltpu.VMEM((128, 128), f32),
            pltpu.VMEM((3, 7, 128, 128), f32),
            pltpu.VMEM((3, 2, 2, 256, 256), bf16),
            *net_scratch(256),
            *net_scratch(256),
            *net_scratch(384),
            pltpu.VMEM((5, 256, 256), bf16),
            pltpu.VMEM((5, 128, 256), f32),
            pltpu.VMEM((5, 256, 384), bf16),
            pltpu.VMEM((5, 128, 384), f32),
            pltpu.VMEM((8, 128), jnp.int32),
            pltpu.VMEM((3, 8, 128), f32),
            pltpu.VMEM((3, 2, 8, 128), f32),
            pltpu.VMEM((16, 128), f32),
            pltpu.VMEM((count, 16, 128), f32),
            pltpu.VMEM((2, count, share, 128), f32),
            pltpu.VMEM((2, count, share, 128), f32),
            pltpu.VMEM((2, share, 128), f32),
            pltpu.VMEM((2, count, share, 128), f32),
            dma((3, 2)),
            dma((3, 2)),
            dma((count,)),
            dma((count,)),
            dma((2, count)),
            dma((2, count)),
            dma((2, count)),
            dma((2, count)),
        ],
        compiler_params=pltpu.CompilerParams(
            collective_id=0, has_side_effects=True, vmem_limit_bytes=64 * 1024 * 1024
        ),
        cost_estimate=pl.CostEstimate(
            flops=3_000_000_000, bytes_accessed=1_000_000, transcendentals=300_000
        ),
    )(*arrays)
    grads = pl.pallas_call(
        finish,
        out_shape=[jax.ShapeDtypeStruct(a.shape, f32) for a in arrays[:12]],
        in_specs=[far] * 12,
        out_specs=[far] * 12,
        scratch_shapes=[*near[:12], dma((12,)), dma((12,))],
        compiler_params=pltpu.CompilerParams(vmem_limit_bytes=64 * 1024 * 1024),
        cost_estimate=pl.CostEstimate(flops=100_000, bytes_accessed=800_000, transcendentals=0),
    )(*results)
    grads = list(grads)
    for k in (0, 4):
        grads[k] = grads[k].transpose(1, 0, 2)
    return tuple(grads)


def on_device(*arrays):
    one_block = arrays[4].shape[0] == 1
    return (fused if one_block else shards)(*arrays)


def solution(mesh):
    placed = (
        P(("groups", "gx"), None, None),
        P(("groups", "gx"), None, None, None),
        P(("groups", "gx"), None, None),
        P(("groups", "gx"), None),
        P("groups", None, None),
        P("groups", None, None, None),
        P("groups", None, None),
        P("groups", None),
        P("groups", None),
        P("groups", None, None),
        P("groups", None),
        P("groups"),
        P(),
        P(("groups", "gx"), None),
        P(("groups", "gx"), None),
        P(("groups", "gx"), None, None),
        P(("groups", "gx"), None),
    )
    return jax.shard_map(
        on_device,
        mesh=mesh,
        in_specs=placed,
        out_specs=(
            P(("groups", "gx"), None, None),
            P(("groups", "gx"), None, None, None),
            P(("groups", "gx"), None, None),
            P(("groups", "gx"), None),
            P("groups", None, None),
            P("groups", None, None, None),
            P("groups", None, None),
            P("groups", None),
            P("groups", None),
            P("groups", None, None),
            P("groups", None),
            P("groups"),
        ),
        check_vma=False,
    )
```
